256 devices in a mesh: dp: 8 (over z), fsdp: 32 (over y, x, core).
Axes of the slice: x: 4, y: 4, z: 8, core: 2. Of those that a mesh axis runs over, the one named last changes fastest.
Arguments:
- tokens: bfloat16 [65536, 8192], P(('dp', 'fsdp')), may hold values from -1.796875 to 1.796875
- gradients: bfloat16 [8, 2, 1024, 8192], P('dp', None, 'fsdp'), may hold values from -1.6953125 to 1.6953125
- weight: bfloat16 [2, 1024, 8192], P(None, 'fsdp'), may hold values from -0.0625 to 0.0625
- owners: int32 [16], replicated, may hold values from 0 to 31, as said below
- counts: int32 [32], replicated, may hold values from 0 to 1, as said below
- left_basis: bfloat16 [32, 1, 1024, 1024], P('fsdp', None, None, 'dp'), may hold values from -0.1875 to 0.1875
- right_basis: bfloat16 [32, 1, 1024, 1024], P('fsdp', None, None, 'dp'), may hold values from -0.1875 to 0.1875
- left_stat: float32 [32, 1, 1024, 1024], P('fsdp', None, None, 'dp'), may hold values from -6 to 6
- right_stat: float32 [32, 1, 1024, 1024], P('fsdp', None, None, 'dp'), may hold values from -6 to 6
- first_moment: bfloat16 [32, 1, 1024, 1024], P('fsdp', None, None, 'dp'), may hold values from -3 to 3
- second_moment: float32 [32, 1, 1024, 1024], P('fsdp', None, None, 'dp'), may hold values from 0.05 to 1
Outputs:
- projected: bfloat16 [65536, 1024], P(('dp', 'fsdp'))
- new_weight: bfloat16 [2, 1024, 8, 1024], P(None, 'fsdp', None, 'dp')
- new_left_stat: float32 [32, 1, 1024, 1024], P('fsdp', None, None, 'dp')
- new_right_stat: float32 [32, 1, 1024, 1024], P('fsdp', None, None, 'dp')
- new_first_moment: bfloat16 [32, 1, 1024, 1024], P('fsdp', None, None, 'dp')
- new_second_moment: float32 [32, 1, 1024, 1024], P('fsdp', None, None, 'dp')
The draws below stay inside these ranges and needn't reach their ends.
Inputs may be any that keep to these rules, and one draw needn't show every extreme that they name: `owners`: no owner holds more than 1 block, and some owner holds exactly 1. counts[o] is the number of blocks whose owner is o.
All inputs are finite; a program needn't handle non-finite values.
Results may differ from the reference program's by a relative error of at most 0.014.
Values may be sent and summed in bfloat16 or wider, within the bound.
No kernel may reach another device: no remote copies, remote signals or barrier semaphores. Data moves between devices by JAX's collectives and lax.ppermute only.
A program may use at most 128 MiB of HBM per device.

```python
import math
import jax
import jax.numpy as jnp
from jax import lax

D = 8192
KV = 1024
BS = 1024
SLOTS = 1
TOKENS = 65536
N_DP = 8
N_FSDP = 32


def assignment(key):
    block_count = 2 * D // BS
    chosen = jax.random.permutation(key, N_FSDP * SLOTS)[:block_count].astype(jnp.int32)
    owner_of = (chosen // SLOTS).astype(jnp.int32)
    held = jnp.sum((owner_of[None, :] == jnp.arange(N_FSDP, dtype=jnp.int32)[:, None]).astype(jnp.int32), axis=1)
    return (owner_of, held.astype(jnp.int32))


def draw_owners(key, part):
    shared = assignment(key)
    return shared[0]


def draw_counts(key, part):
    shared = assignment(key)
    return shared[1]


def levels(rng, dims, split, smallest, top_value):
    factor_of, own = 1.0, jax.random.fold_in(rng, 6)
    for position, parts in split:
        heights = jnp.exp(jax.random.uniform(jax.random.fold_in(own, position), (parts,), jnp.float32, smallest / len(split), top_value / len(split)))
        factor_of = factor_of * jnp.repeat(heights, dims[position] // parts).reshape([-1 if axis == position else 1 for axis in range(len(dims))])
    return factor_of


def centred(rng, dims, spread, limit, split=(), kind=jnp.bfloat16):
    values = spread * jax.random.normal(rng, dims, jnp.float32)
    if split:
        values = values * levels(rng, dims, split, -0.22, 0.18)
    return jnp.clip(values, -limit, limit).astype(kind)


def setup_inputs(seed: int = 0) -> dict:
    splits = jax.random.split(jax.random.key(seed), 12)
    tokens = centred(splits[0], (TOKENS, D), 0.3, 1.796875, ((0, 256),))
    gradients = centred(splits[1], (N_DP, 2, KV, D), 0.28, 1.6953125, ((0, 8), (2, 32)))
    weight = centred(splits[2], (2, KV, D), D ** -0.5, 0.0625, ((1, 32),))
    owners = draw_owners(jax.random.fold_in(splits[11], 71), 0)
    counts = draw_counts(jax.random.fold_in(splits[11], 71), 0)
    left_basis = centred(splits[5], (N_FSDP, SLOTS, BS, BS), BS ** -0.5, 0.1875, ((0, 32), (3, 8)))
    right_basis = centred(splits[6], (N_FSDP, SLOTS, BS, BS), BS ** -0.5, 0.1875, ((0, 32), (3, 8)))
    left_stat = centred(splits[7], (N_FSDP, SLOTS, BS, BS), 1.0, 6.0, ((0, 32), (3, 8)), jnp.float32)
    right_stat = centred(splits[8], (N_FSDP, SLOTS, BS, BS), 1.0, 6.0, ((0, 32), (3, 8)), jnp.float32)
    first_moment = centred(splits[9], (N_FSDP, SLOTS, BS, BS), 0.5, 3.0, ((0, 32), (3, 8)))
    second_moment = jnp.clip(jnp.exp(math.log(1.0) - 2.9957323 * jax.random.uniform(splits[10], (N_FSDP, SLOTS, BS, BS), jnp.float32) ** levels(splits[10], (N_FSDP, SLOTS, BS, BS), ((0, 32), (3, 8)), -0.2, 0.2)), 0.05, 1.0)
    return {"tokens": tokens, "gradients": gradients, "weight": weight, "owners": owners, "counts": counts, "left_basis": left_basis, "right_basis": right_basis, "left_stat": left_stat, "right_stat": right_stat, "first_moment": first_moment, "second_moment": second_moment}


step_size = 0.02
decay_first = 0.9
decay_second = 0.95
decay_gram = 0.95
epsilon = 1e-08

def settle(values):
    return lax.optimization_barrier(values.astype(jnp.bfloat16)).astype(jnp.float32)

def reference(tokens, gradients, weight, owners, counts, left_basis, right_basis, left_stat, right_stat, first_moment, second_moment):
    per_row = D // BS
    block_count = 2 * per_row
    summed = lax.optimization_barrier(jnp.sum(gradients.astype(jnp.float32), axis=0))
    blocks = settle(summed).reshape(2, KV, per_row, BS).transpose(0, 2, 1, 3).reshape(block_count, KV, BS)
    order = jnp.arange(block_count, dtype=jnp.int32)
    same = (owners[None, :] == owners[:, None]) & (order[None, :] < order[:, None])
    places = lax.optimization_barrier(jnp.sum(same.astype(jnp.int32), axis=1)).astype(jnp.int32)
    left_base = left_basis[owners, places].astype(jnp.float32)
    right_base = right_basis[owners, places].astype(jnp.float32)
    gram_left = decay_gram * left_stat[owners, places] + (1.0 - decay_gram) * jnp.einsum('bij,bkj->bik', blocks, blocks)
    gram_right = decay_gram * right_stat[owners, places] + (1.0 - decay_gram) * jnp.einsum('bji,bjk->bik', blocks, blocks)
    rotated = settle(jnp.einsum('bij,bjk->bik', blocks, right_base))
    turned = jnp.einsum('bji,bjk->bik', left_base, rotated)
    moment = decay_first * first_moment[owners, places].astype(jnp.float32) + (1.0 - decay_first) * turned
    second = decay_second * second_moment[owners, places] + (1.0 - decay_second) * turned * turned
    normal = settle(moment / (jnp.sqrt(second) + epsilon))
    back_side = settle(jnp.einsum('bij,bkj->bik', normal, right_base))
    update = settle(jnp.einsum('bij,bjk->bik', left_base, back_side))
    live = jnp.arange(SLOTS, dtype=jnp.int32)[None, :] < counts[:, None]

    def place(older, fresh_values):
        return jnp.where(live[:, :, None, None], older.at[owners, places].set(fresh_values), older)
    new_left_stat = place(left_stat, gram_left)
    new_right_stat = place(right_stat, gram_right)
    new_first_moment = place(first_moment, moment.astype(jnp.bfloat16))
    new_second_moment = place(second_moment, second)
    update_full = update.reshape(2, per_row, KV, BS).transpose(0, 2, 1, 3).reshape(2, KV, D)
    fresh = (weight.astype(jnp.float32) - step_size * update_full).astype(jnp.bfloat16)
    projected = jnp.dot(tokens, fresh[0].T, preferred_element_type=jnp.float32).astype(jnp.bfloat16)
    new_weight = fresh.reshape(2, KV, per_row, BS)
    return (projected, new_weight, new_left_stat, new_right_stat, new_first_moment, new_second_moment)
```

```python
import functools

import jax
import jax.numpy as jnp
from jax import lax
from jax.experimental import pallas as pl
from jax.experimental.pallas import tpu as pltpu
from jax.sharding import PartitionSpec as P

step_size = 0.02
decay_first = 0.9
decay_second = 0.95
decay_gram = 0.95
epsilon = 1e-08

BF = jnp.bfloat16
F32 = jnp.float32
DP = 8
SIDE = 4
CORES = 2
FSDP = SIDE * SIDE * CORES
RING = (0, -1, -2, -3, 4, 1, 2, 3)
COLS_A = (0, -1, 1, -2)
COLS_B = (2, -3, 3, 4)
FOUR = (0, -1, 1, 2)


def params(mebibytes):
    return pltpu.CompilerParams(vmem_limit_bytes=mebibytes << 20)


def cost(flops, moved):
    return pl.CostEstimate(flops=flops, bytes_accessed=moved, transcendentals=0)


def shape(dims, kind=BF):
    return jax.ShapeDtypeStruct(dims, kind)


VM = pl.BlockSpec(memory_space=pltpu.VMEM)
SM = pl.BlockSpec(memory_space=pltpu.SMEM)
HBM = pl.BlockSpec(memory_space=pltpu.HBM)
ANY = pl.BlockSpec(memory_space=pl.ANY)


def along_dp(value, by):
    return lax.ppermute(value, "dp", [(i, (i + by) % DP) for i in range(DP)])


def in_plane(value, axis, by):
    pairs = []
    for i in range(FSDP):
        y, x, c = i // (SIDE * CORES), (i // CORES) % SIDE, i % CORES
        if axis == "x":
            x = (x + by) % SIDE
        elif axis == "y":
            y = (y + by) % SIDE
        else:
            c = (c + by) % CORES
        pairs.append((i, (y * SIDE + x) * CORES + c))
    return lax.ppermute(value, "fsdp", pairs)


def ring_gather(piece, beside):
    up, down, done = [piece], [piece], {}
    for step in range(4):
        if step in beside:
            up[-1], down[-1], done[step] = lax.optimization_barrier(
                (up[-1], down[-1], beside[step])
            )
        up.append(along_dp(up[-1], 1))
        if step < 3:
            down.append(along_dp(down[-1], -1))
    return up + down[1:], done


def four_gather(value, axis):
    half = value.shape[0] // 2
    a, b = in_plane(value, axis, 1), in_plane(value, axis, -1)
    return [value, a, b, in_plane(a[:half], axis, 1), in_plane(b[half:], axis, -1)]


def place_of(offset, rank, count):
    return lax.rem(rank + (offset + count), count)


def lanes(index, width=128):
    return pl.ds(pl.multiple_of(index * width, width), width)


def shares_kernel(wanted, g_ref, *outs):
    d = lax.axis_index("dp")
    for k, out in zip(wanted, outs):
        e = place_of(k, d, DP)
        for b in range(out.shape[0]):
            out[b] = g_ref[b // 8, :, lanes((b % 8) * DP + e)]


def shares(g, wanted):
    rows = g.shape[1]
    return pl.pallas_call(
        functools.partial(shares_kernel, wanted),
        out_shape=[shape((16, rows, 128))] * len(wanted),
        in_specs=[VM],
        out_specs=[VM] * len(wanted),
        compiler_params=params(8),
        cost_estimate=cost(0, 2 << 20),
        name="shares",
    )(g)


def pack_kernel(owners_ref, own_ref, up_ref, down_ref, out_ref):
    out_ref[...] = jnp.zeros_like(out_ref)
    for b in range(own_ref.shape[0]):
        total = own_ref[b].astype(F32) + up_ref[b].astype(F32) + down_ref[b].astype(F32)
        out_ref[owners_ref[b]] = total.astype(BF)


def pack(owners, own, up, down):
    return pl.pallas_call(
        pack_kernel,
        out_shape=shape((FSDP,) + own.shape[1:]),
        in_specs=[SM, VM, VM, VM],
        out_specs=VM,
        compiler_params=params(4),
        cost_estimate=cost(0, 1 << 20),
        name="pack",
    )(owners, own, up, down)


def add(a, b):
    return (a.astype(F32) + b.astype(F32)).astype(BF)


def ring_sum(shares_of, beside):
    up, down, done = shares_of[4], shares_of[5], {}
    for step, (a, b) in enumerate(((3, 6), (2, 7), (1, None))):
        if step in beside:
            up, down, done[step] = lax.optimization_barrier((up, down, beside[step]))
        up, down = add(shares_of[a], along_dp(up, 1)), along_dp(down, -1)
        if b is not None:
            down = add(shares_of[b], down)
    return along_dp(up, 1), down, done


def bring(ref, to, sems, copies):
    copies.append(pltpu.make_async_copy(ref, to, sems.at[len(copies)]))
    copies[-1].start()


def assemble(pieces, out):
    d = lax.axis_index("dp")
    for offset, ref in zip(RING, pieces):
        out[:, lanes(place_of(offset, d, DP))] = ref[...]


def contract(a, b, dims):
    return lax.dot_general(a, b, (dims, ((), ())), preferred_element_type=F32)


def stage_kernel(*refs):
    half = len(refs) // 2
    for ref, out in zip(refs[:half], refs[half:]):
        out[...] = ref[...]


def stage(*arrays):
    return pl.pallas_call(
        stage_kernel,
        out_shape=[shape(v.shape, v.dtype) for v in arrays],
        in_specs=[VM] * len(arrays),
        out_specs=[VM] * len(arrays),
        compiler_params=params(8),
        cost_estimate=cost(0, 6 << 20),
        name="stage",
    )(*arrays)


def moments_kernel(live_ref, *refs):
    pieces, (left_ref, right_ref, first_ref, second_ref) = refs[:8], refs[8:12]
    m_ref, v_ref, ln_ref, up_ref, down_ref, g_ref = refs[12:]
    assemble(pieces, g_ref)
    rotated = contract(g_ref[...], right_ref[...], ((1,), (0,))).astype(BF)
    turned = contract(left_ref[...], rotated, ((0,), (0,)))
    moment = decay_first * first_ref[...].astype(F32) + (1.0 - decay_first) * turned
    second = decay_second * second_ref[...] + (1.0 - decay_second) * turned * turned
    normal = (moment / (jnp.sqrt(second) + epsilon)).astype(BF)
    back = contract(left_ref[...], normal, ((1,), (0,))).astype(BF)
    ln_ref[...] = back
    back_share(back, right_ref, 4, up_ref)
    back_share(back, right_ref, 5, down_ref)
    live = live_ref[0] > 0
    m_ref[...] = jnp.where(live, moment.astype(BF), first_ref[...])
    v_ref[...] = jnp.where(live, second, second_ref[...])


def back_share(back, right_ref, distance, out):
    rows = lanes(place_of(distance, lax.axis_index("dp"), DP))
    out[...] = contract(back, right_ref[rows, :], ((1,), (1,))).astype(BF)


def moments(live, pieces, left, right, first, second):
    size, share = right.shape
    kinds = (BF, F32, BF, BF, BF)
    return pl.pallas_call(
        moments_kernel,
        out_shape=[shape((size, share), kind) for kind in kinds],
        in_specs=[SM] + [VM] * 12,
        out_specs=[VM] * 5,
        scratch_shapes=[pltpu.VMEM((size, size), BF)],
        compiler_params=params(20),
        cost_estimate=cost(6 * size * size * share, 7 << 20),
        name="moments",
    )(live, *pieces, left, right, first, second)


LATER = (3, 6, 2, 7, 1, 0)


def later_kernel(ln_ref, right_ref, *outs):
    for distance, out in zip(LATER, outs):
        back_share(ln_ref[...], right_ref, distance, out)


def later_shares(back, right):
    return pl.pallas_call(
        later_kernel,
        out_shape=[shape(back.shape)] * len(LATER),
        in_specs=[VM] * 2,
        out_specs=[VM] * len(LATER),
        compiler_params=params(8),
        cost_estimate=cost(2 * back.shape[0] ** 2 * back.shape[1], 2 << 20),
        name="later_shares",
    )(back, right)


def grams_kernel(live_ref, *refs):
    pieces = refs[:8]
    left_ref, right_ref, new_left_ref, new_right_ref, g_ref = refs[8:]
    assemble(pieces, g_ref)
    d = lax.axis_index("dp")
    live = live_ref[0] > 0
    gram = contract(g_ref[...], g_ref[lanes(d), :], ((1,), (1,)))
    old = left_ref[...]
    new_left_ref[...] = jnp.where(live, decay_gram * old + (1.0 - decay_gram) * gram, old)
    gram = contract(g_ref[...], pieces[0][...], ((0,), (0,)))
    old = right_ref[...]
    new_right_ref[...] = jnp.where(live, decay_gram * old + (1.0 - decay_gram) * gram, old)


def grams(live, pieces, left_stat, right_stat):
    size, share = left_stat.shape
    return pl.pallas_call(
        grams_kernel,
        out_shape=[shape((size, share), F32)] * 2,
        in_specs=[SM] + [VM] * 10,
        out_specs=[VM] * 2,
        scratch_shapes=[pltpu.VMEM((size, size), BF)],
        compiler_params=params(20),
        cost_estimate=cost(4 * size * size * share, 5 << 20),
        name="grams",
    )(live, *pieces, left_stat, right_stat)


def fresh_kernel(owners_ref, weight_ref, back_ref, new_ref, key_ref):
    d = lax.axis_index("dp")
    for b in range(new_ref.shape[0]):
        old = weight_ref[b // 8, :, lanes((b % 8) * DP + d)].astype(F32)
        value = (old - step_size * back_ref[owners_ref[b]].astype(F32)).astype(BF)
        new_ref[b] = value
        if b < 8:
            key_ref[:, b * 128 : (b + 1) * 128] = value


def fresh_rows(owners, weight, back):
    rows = weight.shape[1]
    return pl.pallas_call(
        fresh_kernel,
        out_shape=[shape((16, rows, 128)), shape((rows, 1024))],
        in_specs=[SM, VM, VM],
        out_specs=[VM, VM],
        compiler_params=params(8),
        cost_estimate=cost(0, 2 << 20),
        name="fresh_rows",
    )(owners, weight, back)


def order_kernel(t_ref, a_ref, b_ref):
    d = lax.axis_index("dp")
    for offsets, out in ((COLS_A, a_ref), (COLS_B, b_ref)):
        for q, offset in enumerate(offsets):
            e = place_of(offset, d, DP)
            for c in range(8):
                at = (q * 8 + c) * 128
                out[:, at : at + 128] = t_ref[:, lanes(c * DP + e)]


def order_tokens(tokens):
    count, width = tokens.shape
    return pl.pallas_call(
        order_kernel,
        grid=(2,),
        out_shape=[shape((count, width // 2))] * 2,
        in_specs=[pl.BlockSpec((count // 2, width), lambda i: (i, 0))],
        out_specs=[pl.BlockSpec((count // 2, width // 2), lambda i: (i, 0))] * 2,
        compiler_params=params(12),
        cost_estimate=cost(0, 8 << 20),
        name="order_tokens",
    )(tokens)


def project_kernel(*refs):
    a_refs, b_refs = refs[:5], refs[5:10]
    own_a, own_b, other_a, other_b, own_out, other_out, keys, sems = refs[10:]
    rank = lax.axis_index("fsdp")
    y, x = lax.div(rank, SIDE * CORES), lax.rem(lax.div(rank, CORES), SIDE)
    half = own_a.shape[1]
    copies = []

    def bring(ref, row, place, column):
        to = keys.at[pl.ds(pl.multiple_of(place * 32, 32), 32), column : column + half]
        copy = pltpu.make_async_copy(ref.at[row : row + 32, :], to, sems.at[len(copies)])
        copy.start()
        copies.append(copy)

    for refs_of, column, first_y in ((a_refs, 0, True), (b_refs, half, False)):
        for i in range(16):
            far, near = FOUR[i // 4], FOUR[i % 4]
            if first_y:
                place = place_of(far, y, SIDE) * SIDE + place_of(near, x, SIDE)
            else:
                place = place_of(near, y, SIDE) * SIDE + place_of(far, x, SIDE)
            which = i // 4 if i < 12 else 3 + (i - 12) // 2
            row = (i % 4) * 32 if i < 12 else (i % 2) * 32
            bring(refs_of[which], row, place, column)
    for copy in copies:
        copy.wait()
    for n in range(0, keys.shape[0], 256):
        for tok_a, tok_b, out in ((own_a, own_b, own_out), (other_a, other_b, other_out)):
            value = contract(tok_a[...], keys[n : n + 256, :half], ((1,), (1,)))
            value += contract(tok_b[...], keys[n : n + 256, half:], ((1,), (1,)))
            out[:, n : n + 256] = value.astype(BF)


def project(a, b, own, other):
    count, half = own[0].shape
    size = SIDE * SIDE * 32
    return pl.pallas_call(
        project_kernel,
        out_shape=[shape((count, size))] * 2,
        in_specs=[ANY] * 10 + [VM] * 4,
        out_specs=[VM] * 2,
        scratch_shapes=[pltpu.VMEM((size, 2 * half), BF), pltpu.SemaphoreType.DMA((32,))],
        compiler_params=params(28),
        cost_estimate=cost(8 * count * half * size, 20 << 20),
        name="project",
    )(*a, *b, *own, *other)


def on_device(
    tokens,
    gradients,
    weight,
    owners,
    counts,
    left_basis,
    right_basis,
    left_stat,
    right_stat,
    first_moment,
    second_moment,
):
    fsdp_rank = lax.axis_index("fsdp")
    row_share = weight.shape[1]
    block_size, col_share = left_basis.shape[2:]
    live = lax.dynamic_slice_in_dim(counts, fsdp_rank, 1)
    left_local, right_local = left_basis[0, 0], right_basis[0, 0]

    left_full = lax.all_gather(left_local, "dp", axis=1, tiled=True)
    grad = gradients[0]
    shares_of = dict(zip((4, 5), shares(grad, (4, 5))))
    shares_of.update(zip(LATER, shares(grad, LATER)))
    up, down, done = ring_sum(shares_of, {1: tokens})
    packed = pack(owners, shares_of[0], up, down)
    own = order_tokens(done[1])
    other = [in_plane(v, "core", 1) for v in own]

    arrived = lax.all_to_all(packed, "fsdp", split_axis=0, concat_axis=0, tiled=True)
    arrived = arrived.reshape(block_size, col_share)
    state = stage(right_local, first_moment[0, 0], second_moment[0, 0])
    pieces, done = ring_gather(arrived, {1: left_full, 2: (own, other), 3: state})
    (own, other), left_full, (right, first, second) = done[2], done[1], done[3]
    new_first, new_second, back, *ends = moments(live, pieces, left_full, right, first, second)
    shares_of = dict(zip((4, 5), ends))
    shares_of.update(zip(LATER, later_shares(back, right)))
    stats = grams(live, pieces, left_stat[0, 0], right_stat[0, 0])
    up, down, done = ring_sum(shares_of, {2: tuple(stats)})
    new_left, new_right = done[2]
    update = (shares_of[0].astype(F32) + up.astype(F32) + down.astype(F32)).astype(BF)
    returned = lax.all_to_all(
        update.reshape(FSDP, row_share, col_share), "fsdp", split_axis=0, concat_axis=0, tiled=True
    )
    new_rows, key_rows = fresh_rows(owners, weight, returned)
    new_weight = new_rows.reshape(2, 8, row_share, col_share).transpose(0, 2, 1, 3)

    held = dict(zip(RING, ring_gather(key_rows, {})[0]))
    part_a = jnp.concatenate([held[k] for k in COLS_A], 1)
    part_b = jnp.concatenate([held[k] for k in COLS_B], 1)
    part_a = jnp.concatenate(four_gather(part_a, "x"), 0)
    part_b = jnp.concatenate(four_gather(part_b, "y"), 0)
    part_a, part_b = lax.optimization_barrier((part_a, part_b))
    part_a, part_b = four_gather(part_a, "y"), four_gather(part_b, "x")
    mine, theirs = project(part_a, part_b, own, other)
    got = in_plane(theirs, "core", 1)
    core = lax.rem(fsdp_rank, CORES)
    even = jnp.where(core == 0, mine, got)
    odd = jnp.where(core == 0, got, mine)
    count = tokens.shape[0]
    projected = jnp.stack(
        [even.reshape(count, SIDE * SIDE, row_share), odd.reshape(count, SIDE * SIDE, row_share)], 2
    ).reshape(count, SIDE * SIDE * CORES * row_share)
    return (
        projected,
        new_weight,
        new_left[None, None],
        new_right[None, None],
        new_first[None, None],
        new_second[None, None],
    )


def solution(mesh):
    state = P("fsdp", None, None, "dp")
    return jax.shard_map(
        on_device,
        mesh=mesh,
        in_specs=(
            P(("dp", "fsdp"), None),
            P("dp", None, "fsdp", None),
            P(None, "fsdp", None),
            P(),
            P(),
            state,
            state,
            state,
            state,
            state,
            state,
        ),
        out_specs=(
            P(("dp", "fsdp"), None),
            P(None, "fsdp", None, "dp"),
            state,
            state,
            state,
            state,
        ),
        check_vma=False,
    )
```

```python
import functools

import jax
import jax.numpy as jnp
from jax import lax
from jax.experimental import pallas as pl
from jax.experimental.pallas import tpu as pltpu
from jax.sharding import PartitionSpec as P

step_size = 0.02
decay_first = 0.9
decay_second = 0.95
decay_gram = 0.95
epsilon = 1e-08

BF = jnp.bfloat16
F32 = jnp.float32
DP = 8
SIDE = 4
CORES = 2
FSDP = SIDE * SIDE * CORES
RING = (0, -1, -2, -3, 4, 1, 2, 3)
FOUR = (0, -1, 1, 2)


def params(mebibytes):
    return pltpu.CompilerParams(vmem_limit_bytes=mebibytes << 20)


def cost(flops, moved):
    return pl.CostEstimate(flops=flops, bytes_accessed=moved, transcendentals=0)


def shape(dims, kind=BF):
    return jax.ShapeDtypeStruct(dims, kind)


VM = pl.BlockSpec(memory_space=pltpu.VMEM)
SM = pl.BlockSpec(memory_space=pltpu.SMEM)
HBM = pl.BlockSpec(memory_space=pltpu.HBM)
ANY = pl.BlockSpec(memory_space=pl.ANY)


def along_dp(value, by):
    return lax.ppermute(value, "dp", [(i, (i + by) % DP) for i in range(DP)])


def in_plane(value, axis, by):
    pairs = []
    for i in range(FSDP):
        y, x, c = i // (SIDE * CORES), (i // CORES) % SIDE, i % CORES
        if axis == "x":
            x = (x + by) % SIDE
        elif axis == "y":
            y = (y + by) % SIDE
        else:
            c = (c + by) % CORES
        pairs.append((i, (y * SIDE + x) * CORES + c))
    return lax.ppermute(value, "fsdp", pairs)


def ring_gather(piece, beside):
    up, down, done = [piece], [piece], {}
    for step in range(4):
        if step in beside:
            up[-1], down[-1], done[step] = lax.optimization_barrier(
                (up[-1], down[-1], beside[step])
            )
        up.append(along_dp(up[-1], 1))
        if step < 3:
            down.append(along_dp(down[-1], -1))
    return up + down[1:], done


def four_gather(value, axis):
    half = value.shape[0] // 2
    a, b = in_plane(value, axis, 1), in_plane(value, axis, -1)
    return [value, a, b, in_plane(a[:half], axis, 1), in_plane(b[half:], axis, -1)]


def place_of(offset, rank, count):
    return lax.rem(rank + (offset + count), count)


def lanes(index, width=128):
    return pl.ds(pl.multiple_of(index * width, width), width)


def shares_kernel(wanted, g_ref, *outs):
    d = lax.axis_index("dp")
    for k, out in zip(wanted, outs):
        e = place_of(k, d, DP)
        for b in range(out.shape[0]):
            out[b] = g_ref[b // 8, :, lanes((b % 8) * DP + e)]


def shares(g, wanted):
    rows = g.shape[1]
    return pl.pallas_call(
        functools.partial(shares_kernel, wanted),
        out_shape=[shape((16, rows, 128))] * len(wanted),
        in_specs=[VM],
        out_specs=[VM] * len(wanted),
        compiler_params=params(8),
        cost_estimate=cost(0, 2 << 20),
        name="shares",
    )(g)


def pack_kernel(owners_ref, own_ref, up_ref, down_ref, out_ref):
    out_ref[...] = jnp.zeros_like(out_ref)
    for b in range(own_ref.shape[0]):
        total = own_ref[b].astype(F32) + up_ref[b].astype(F32) + down_ref[b].astype(F32)
        out_ref[owners_ref[b]] = total.astype(BF)


def pack(owners, own, up, down):
    return pl.pallas_call(
        pack_kernel,
        out_shape=shape((FSDP,) + own.shape[1:]),
        in_specs=[SM, VM, VM, VM],
        out_specs=VM,
        compiler_params=params(4),
        cost_estimate=cost(0, 1 << 20),
        name="pack",
    )(owners, own, up, down)


def add(a, b):
    return (a.astype(F32) + b.astype(F32)).astype(BF)


def ring_sum(shares_of, beside):
    up, down, done = shares_of[4], shares_of[5], {}
    for step, (a, b) in enumerate(((3, 6), (2, 7), (1, None))):
        if step in beside:
            up, down, done[step] = lax.optimization_barrier((up, down, beside[step]))
        up, down = add(shares_of[a], along_dp(up, 1)), along_dp(down, -1)
        if b is not None:
            down = add(shares_of[b], down)
    return along_dp(up, 1), down, done


def bring(ref, to, sems, copies):
    copies.append(pltpu.make_async_copy(ref, to, sems.at[len(copies)]))
    copies[-1].start()


def assemble(pieces, out):
    d = lax.axis_index("dp")
    for offset, ref in zip(RING, pieces):
        out[:, lanes(place_of(offset, d, DP))] = ref[...]


def contract(a, b, dims):
    return lax.dot_general(a, b, (dims, ((), ())), preferred_element_type=F32)


def stage_kernel(*refs):
    pieces, others, (left_ref, *outs) = refs[:8], refs[8:11], refs[11:]
    assemble(pieces, left_ref)
    for ref, out in zip(others, outs):
        out[...] = ref[...]


def stage(pieces, *others):
    size = pieces[0].shape[0]
    return pl.pallas_call(
        stage_kernel,
        out_shape=[shape((size, size))] + [shape(v.shape, v.dtype) for v in others],
        in_specs=[VM] * 11,
        out_specs=[VM] * 4,
        compiler_params=params(12),
        cost_estimate=cost(0, 6 << 20),
        name="stage",
    )(*pieces, *others)


def is_live(counts_ref):
    return counts_ref[lax.axis_index("fsdp")] > 0


def moments_kernel(counts_ref, *refs):
    pieces, (left_ref, right_ref, first_ref, second_ref) = refs[:8], refs[8:12]
    m_ref, v_ref, ln_ref, up_ref, down_ref, g_ref = refs[12:]
    assemble(pieces, g_ref)
    rotated = contract(g_ref[...], right_ref[...], ((1,), (0,))).astype(BF)
    turned = contract(left_ref[...], rotated, ((0,), (0,)))
    moment = decay_first * first_ref[...].astype(F32) + (1.0 - decay_first) * turned
    second = decay_second * second_ref[...] + (1.0 - decay_second) * turned * turned
    normal = (moment / (jnp.sqrt(second) + epsilon)).astype(BF)
    back = contract(left_ref[...], normal, ((1,), (0,))).astype(BF)
    ln_ref[...] = back
    back_share(back, right_ref, 4, up_ref)
    back_share(back, right_ref, 5, down_ref)
    live = is_live(counts_ref)
    m_ref[...] = jnp.where(live, moment.astype(BF), first_ref[...])
    v_ref[...] = jnp.where(live, second, second_ref[...])


def back_share(back, right_ref, distance, out):
    rows = lanes(place_of(distance, lax.axis_index("dp"), DP))
    out[...] = contract(back, right_ref[rows, :], ((1,), (1,))).astype(BF)


def moments(counts, pieces, left, right, first, second):
    size, share = right.shape
    kinds = (BF, F32, BF, BF, BF)
    return pl.pallas_call(
        moments_kernel,
        out_shape=[shape((size, share), kind) for kind in kinds],
        in_specs=[SM] + [VM] * 12,
        out_specs=[VM] * 5,
        scratch_shapes=[pltpu.VMEM((size, size), BF)],
        compiler_params=params(20),
        cost_estimate=cost(6 * size * size * share, 7 << 20),
        name="moments",
    )(counts, *pieces, left, right, first, second)


LATER = (3, 6, 2, 7, 1, 0)


def later_kernel(ln_ref, right_ref, *outs):
    for distance, out in zip(LATER, outs):
        back_share(ln_ref[...], right_ref, distance, out)


def later_shares(back, right):
    return pl.pallas_call(
        later_kernel,
        out_shape=[shape(back.shape)] * len(LATER),
        in_specs=[VM] * 2,
        out_specs=[VM] * len(LATER),
        compiler_params=params(8),
        cost_estimate=cost(2 * back.shape[0] ** 2 * back.shape[1], 2 << 20),
        name="later_shares",
    )(back, right)


def grams_kernel(counts_ref, *refs):
    pieces = refs[:8]
    left_ref, right_ref, new_left_ref, new_right_ref, g_ref = refs[8:]
    assemble(pieces, g_ref)
    d = lax.axis_index("dp")
    live = is_live(counts_ref)
    gram = contract(g_ref[...], g_ref[lanes(d), :], ((1,), (1,)))
    old = left_ref[...]
    new_left_ref[...] = jnp.where(live, decay_gram * old + (1.0 - decay_gram) * gram, old)
    gram = contract(g_ref[...], pieces[0][...], ((0,), (0,)))
    old = right_ref[...]
    new_right_ref[...] = jnp.where(live, decay_gram * old + (1.0 - decay_gram) * gram, old)


def grams(counts, pieces, left_stat, right_stat):
    size, share = left_stat.shape
    return pl.pallas_call(
        grams_kernel,
        out_shape=[shape((size, share), F32)] * 2,
        in_specs=[SM] + [VM] * 10,
        out_specs=[VM] * 2,
        scratch_shapes=[pltpu.VMEM((size, size), BF)],
        compiler_params=params(20),
        cost_estimate=cost(4 * size * size * share, 5 << 20),
        name="grams",
    )(counts, *pieces, left_stat, right_stat)


def fresh_kernel(owners_ref, weight_ref, back_ref, new_ref, key_ref):
    d = lax.axis_index("dp")
    for b in range(new_ref.shape[0]):
        old = weight_ref[b // 8, :, lanes((b % 8) * DP + d)].astype(F32)
        value = (old - step_size * back_ref[owners_ref[b]].astype(F32)).astype(BF)
        new_ref[b] = value
        if b < 8:
            key_ref[:, b * 128 : (b + 1) * 128] = value


def fresh_rows(owners, weight, back):
    rows = weight.shape[1]
    return pl.pallas_call(
        fresh_kernel,
        out_shape=[shape((16, rows, 128)), shape((rows, 1024))],
        in_specs=[SM, VM, VM],
        out_specs=[VM, VM],
        compiler_params=params(8),
        cost_estimate=cost(0, 2 << 20),
        name="fresh_rows",
    )(owners, weight, back)


def lay_kernel(*refs):
    pieces, outs = refs[:8], refs[8:]
    d = lax.axis_index("dp")
    for offset, ref in zip(RING, pieces):
        e = place_of(offset, d, DP)
        for c in range(8):
            outs[c // 4][:, lanes((c % 4) * DP + e)] = ref[:, c * 128 : (c + 1) * 128]


def lay(pieces):
    rows, wide = pieces[0].shape
    return pl.pallas_call(
        lay_kernel,
        out_shape=[shape((rows, 4 * wide))] * 2,
        in_specs=[VM] * 8,
        out_specs=[VM] * 2,
        compiler_params=params(4),
        cost_estimate=cost(0, 1 << 20),
        name="lay",
    )(*pieces)


def here():
    rank = lax.axis_index("fsdp")
    return lax.div(rank, SIDE * CORES), lax.rem(lax.div(rank, CORES), SIDE)


def rows_of(place, count=32):
    return pl.ds(pl.multiple_of(place * count, count), count)


def project_near_kernel(*refs):
    a_refs, b_refs, tokens, outs, keys, sems = refs[:3], refs[3:6], refs[6:8], refs[8:10], *refs[10:]
    y, x = here()
    half = keys.shape[1] // 2
    copies = []
    for i, far in enumerate(FOUR[:3]):
        for j, near in enumerate(FOUR):
            place = place_of(far, y, SIDE) * SIDE + place_of(near, x, SIDE)
            to = keys.at[rows_of(place), :half]
            bring(a_refs[i].at[j * 32 : j * 32 + 32, :], to, sems, copies)
            place = place_of(near, y, SIDE) * SIDE + place_of(far, x, SIDE)
            to = keys.at[rows_of(place), half:]
            bring(b_refs[i].at[j * 32 : j * 32 + 32, :], to, sems, copies)
    nothing = jnp.zeros((32, half), BF)
    for j in range(SIDE):
        keys[rows_of(place_of(2, y, SIDE) * SIDE + j), :half] = nothing
        keys[rows_of(j * SIDE + place_of(2, x, SIDE)), half:] = nothing
    for copy in copies:
        copy.wait()
    for n in range(0, keys.shape[0], 256):
        for ref, out in zip(tokens, outs):
            out[:, n : n + 256] = contract(ref[...], keys[n : n + 256, :], ((1,), (1,)))


def project_near(a, b, tokens):
    count, width = tokens[0].shape
    size = SIDE * SIDE * 32
    return pl.pallas_call(
        project_near_kernel,
        out_shape=[shape((count, size), F32)] * 2,
        in_specs=[ANY] * 6 + [VM] * 2,
        out_specs=[VM] * 2,
        scratch_shapes=[pltpu.VMEM((size, width), BF), pltpu.SemaphoreType.DMA((24,))],
        compiler_params=params(22),
        cost_estimate=cost(4 * count * width * size, 16 << 20),
        name="project_near",
    )(*a, *b, *tokens)


def project_far_kernel(*refs):
    far, tokens, sums, outs, (keys_a, keys_b) = refs[:4], refs[4:6], refs[6:8], refs[8:10], refs[10:]
    y, x = here()
    half = keys_a.shape[1]
    for rank, keys, parts in ((x, keys_a, far[:2]), (y, keys_b, far[2:])):
        for j, offset in enumerate(FOUR):
            row = (j % 2) * 32
            keys[rows_of(place_of(offset, rank, SIDE)), :] = parts[j // 2][row : row + 32, :]
    lane = lax.broadcasted_iota(jnp.int32, (tokens[0].shape[0], 128), 1)
    far_y, far_x = place_of(2, y, SIDE), place_of(2, x, SIDE)
    wanted = lax.div(lane, 32) == far_x
    for ref, total, out in zip(tokens, sums, outs):
        by_x = contract(ref[:, :half], keys_a[...], ((1,), (1,)))
        by_y = contract(ref[:, half:], keys_b[...], ((1,), (1,)))
        for j in range(SIDE):
            moved = pltpu.roll(by_y, lax.rem(far_x + (SIDE - j), SIDE) * 32, 1)
            value = total[:, j * 128 : j * 128 + 128] + jnp.where(wanted, moved, 0.0)
            value += jnp.where(far_y == j, by_x, 0.0)
            out[:, j * 128 : j * 128 + 128] = value.astype(BF)


def project_far(far, tokens, sums):
    count, width = tokens[0].shape
    size = sums[0].shape[1]
    return pl.pallas_call(
        project_far_kernel,
        out_shape=[shape((count, size))] * 2,
        in_specs=[VM] * 8,
        out_specs=[VM] * 2,
        scratch_shapes=[pltpu.VMEM((128, width // 2), BF)] * 2,
        compiler_params=params(16),
        cost_estimate=cost(count * width * size, 4 << 20),
        name="project_far",
    )(*far, *tokens, *sums)


def on_device(
    tokens,
    gradients,
    weight,
    owners,
    counts,
    left_basis,
    right_basis,
    left_stat,
    right_stat,
    first_moment,
    second_moment,
):
    row_share = weight.shape[1]
    block_size, col_share = left_basis.shape[2:]
    left_local, right_local = left_basis[0, 0], right_basis[0, 0]

    grad = gradients[0]
    shares_of = dict(zip((4, 5), shares(grad, (4, 5))))
    shares_of.update(zip(LATER, shares(grad, LATER)))
    first_left = along_dp(left_local, 1), along_dp(left_local, -1)
    up, down, done = ring_sum(shares_of, {2: first_left})
    first_left = done[2]
    second_left = along_dp(first_left[0], 1), along_dp(first_left[1], -1)
    up, down, second_left = lax.optimization_barrier((up, down, second_left))
    third_left = along_dp(second_left[0], 1), along_dp(second_left[1], -1)
    packed = pack(owners, shares_of[0], up, down)

    arrived = lax.all_to_all(packed, "fsdp", split_axis=0, concat_axis=0, tiled=True)
    arrived = arrived.reshape(block_size, col_share)
    last_left = along_dp(third_left[0], 1)
    pieces, done = ring_gather(arrived, {1: third_left, 3: last_left})
    lefts = [left_local, first_left[0], second_left[0], done[1][0], done[3]]
    lefts += [first_left[1], second_left[1], done[1][1]]
    left_full, right, first, second = stage(
        lefts, right_local, first_moment[0, 0], second_moment[0, 0]
    )
    new_first, new_second, back, *ends = moments(counts, pieces, left_full, right, first, second)
    shares_of = dict(zip((4, 5), ends))
    shares_of.update(zip(LATER, later_shares(back, right)))
    up, down, done = ring_sum(shares_of, {1: in_plane(tokens, "core", 1)})
    other = done[1]
    update = (shares_of[0].astype(F32) + up.astype(F32) + down.astype(F32)).astype(BF)
    returned = lax.all_to_all(
        update.reshape(FSDP, row_share, col_share), "fsdp", split_axis=0, concat_axis=0, tiled=True
    )
    new_rows, key_rows = fresh_rows(owners, weight, returned)
    new_weight = new_rows.reshape(2, 8, row_share, col_share).transpose(0, 2, 1, 3)

    part_a, part_b = lay(ring_gather(key_rows, {})[0])
    part_a = jnp.concatenate(four_gather(part_a, "x"), 0)
    part_b = jnp.concatenate(four_gather(part_b, "y"), 0)
    part_a, part_b = lax.optimization_barrier((part_a, part_b))
    stats = grams(counts, pieces, left_stat[0, 0], right_stat[0, 0])
    near_a = in_plane(part_a, "y", 1), in_plane(part_a, "y", -1)
    near_b = in_plane(part_b, "x", 1), in_plane(part_b, "x", -1)
    near_a, near_b, stats = lax.optimization_barrier((near_a, near_b, stats))
    new_left, new_right = stats
    half = part_a.shape[0] // 2
    far_a = in_plane(near_a[0][:half], "y", 1), in_plane(near_a[1][half:], "y", -1)
    far_b = in_plane(near_b[0][:half], "x", 1), in_plane(near_b[1][half:], "x", -1)
    tokens = (tokens, other)
    sums = project_near((part_a, *near_a), (part_b, *near_b), tokens)
    mine, theirs = project_far((*far_a, *far_b), tokens, sums)
    got = in_plane(theirs, "core", 1)
    core = lax.rem(lax.axis_index("fsdp"), CORES)
    even = jnp.where(core == 0, mine, got)
    odd = jnp.where(core == 0, got, mine)
    count = tokens[0].shape[0]
    projected = jnp.stack(
        [even.reshape(count, SIDE * SIDE, row_share), odd.reshape(count, SIDE * SIDE, row_share)], 2
    ).reshape(count, SIDE * SIDE * CORES * row_share)
    return (
        projected,
        new_weight,
        new_left[None, None],
        new_right[None, None],
        new_first[None, None],
        new_second[None, None],
    )


def solution(mesh):
    state = P("fsdp", None, None, "dp")
    return jax.shard_map(
        on_device,
        mesh=mesh,
        in_specs=(
            P(("dp", "fsdp"), None),
            P("dp", None, "fsdp", None),
            P(None, "fsdp", None),
            P(),
            P(),
            state,
            state,
            state,
            state,
            state,
            state,
        ),
        out_specs=(
            P(("dp", "fsdp"), None),
            P(None, "fsdp", None, "dp"),
            state,
            state,
            state,
            state,
        ),
        check_vma=False,
    )
```

```python
import functools

import jax
import jax.numpy as jnp
from jax import lax
from jax.experimental import pallas as pl
from jax.experimental.pallas import tpu as pltpu
from jax.sharding import PartitionSpec as P

step_size = 0.02
decay_first = 0.9
decay_second = 0.95
decay_gram = 0.95
epsilon = 1e-08

BF = jnp.bfloat16
F32 = jnp.float32
DP = 8
SIDE = 4
CORES = 2
FSDP = SIDE * SIDE * CORES
RING = (0, -1, -2, -3, 4, 1, 2, 3)
FOUR = (0, -1, 1, 2)


def params(mebibytes):
    return pltpu.CompilerParams(vmem_limit_bytes=mebibytes << 20)


def cost(flops, moved):
    return pl.CostEstimate(flops=flops, bytes_accessed=moved, transcendentals=0)


def shape(dims, kind=BF):
    return jax.ShapeDtypeStruct(dims, kind)


VM = pl.BlockSpec(memory_space=pltpu.VMEM)
SM = pl.BlockSpec(memory_space=pltpu.SMEM)
HBM = pl.BlockSpec(memory_space=pltpu.HBM)
ANY = pl.BlockSpec(memory_space=pl.ANY)


def along_dp(value, by):
    return lax.ppermute(value, "dp", [(i, (i + by) % DP) for i in range(DP)])


def in_plane(value, axis, by):
    pairs = []
    for i in range(FSDP):
        y, x, c = i // (SIDE * CORES), (i // CORES) % SIDE, i % CORES
        if axis == "x":
            x = (x + by) % SIDE
        elif axis == "y":
            y = (y + by) % SIDE
        else:
            c = (c + by) % CORES
        pairs.append((i, (y * SIDE + x) * CORES + c))
    return lax.ppermute(value, "fsdp", pairs)


def ring_gather(piece, beside):
    up, down, done = [piece], [piece], {}
    for step in range(4):
        if step in beside:
            up[-1], down[-1], done[step] = lax.optimization_barrier(
                (up[-1], down[-1], beside[step])
            )
        up.append(along_dp(up[-1], 1))
        if step > 0:
            down.append(along_dp(down[-1], -1))
    return up + down[1:], done


def four_gather(value, axis):
    half = value.shape[0] // 2
    a, b = in_plane(value, axis, 1), in_plane(value, axis, -1)
    return [value, a, b, in_plane(a[:half], axis, 1), in_plane(b[half:], axis, -1)]


def place_of(offset, rank, count):
    return lax.rem(rank + (offset + count), count)


def lanes(index, width=128):
    return pl.ds(pl.multiple_of(index * width, width), width)


def shares_kernel(wanted, g_ref, *outs):
    d = lax.axis_index("dp")
    for k, out in zip(wanted, outs):
        e = place_of(k, d, DP)
        for b in range(out.shape[0]):
            out[b] = g_ref[b // 8, :, lanes((b % 8) * DP + e)]


def shares(g, wanted):
    rows = g.shape[1]
    return pl.pallas_call(
        functools.partial(shares_kernel, wanted),
        out_shape=[shape((16, rows, 128))] * len(wanted),
        in_specs=[VM],
        out_specs=[VM] * len(wanted),
        compiler_params=params(8),
        cost_estimate=cost(0, 2 << 20),
        name="shares",
    )(g)


def pack_kernel(owners_ref, own_ref, up_ref, down_ref, out_ref):
    out_ref[...] = jnp.zeros_like(out_ref)
    for b in range(own_ref.shape[0]):
        total = own_ref[b].astype(F32) + up_ref[b].astype(F32) + down_ref[b].astype(F32)
        out_ref[owners_ref[b]] = total.astype(BF)


def pack(owners, own, up, down):
    return pl.pallas_call(
        pack_kernel,
        out_shape=shape((FSDP,) + own.shape[1:]),
        in_specs=[SM, VM, VM, VM],
        out_specs=VM,
        compiler_params=params(4),
        cost_estimate=cost(0, 1 << 20),
        name="pack",
    )(owners, own, up, down)


def add(a, b):
    return (a.astype(F32) + b.astype(F32)).astype(BF)


def ring_sum(shares_of, beside):
    up, down, done = add(shares_of[3], along_dp(shares_of[4], 1)), shares_of[5], {}
    for step, a, b in ((1, 2, 6), (2, 1, 7), (3, None, None)):
        if step in beside:
            up, down, done[step] = lax.optimization_barrier((up, down, beside[step]))
        up, down = along_dp(up, 1), along_dp(down, -1)
        if a is not None:
            up, down = add(shares_of[a], up), add(shares_of[b], down)
    return up, down, done


def bring(ref, to, sems, copies):
    copies.append(pltpu.make_async_copy(ref, to, sems.at[len(copies)]))
    copies[-1].start()


def assemble(pieces, out):
    d = lax.axis_index("dp")
    for offset, ref in zip(RING, pieces):
        out[:, lanes(place_of(offset, d, DP))] = ref[...]


def contract(a, b, dims):
    return lax.dot_general(a, b, (dims, ((), ())), preferred_element_type=F32)


def stage_kernel(*refs):
    pieces, others, (left_ref, *outs) = refs[:8], refs[8:11], refs[11:]
    assemble(pieces, left_ref)
    for ref, out in zip(others, outs):
        out[...] = ref[...]


def stage(pieces, *others):
    size = pieces[0].shape[0]
    return pl.pallas_call(
        stage_kernel,
        out_shape=[shape((size, size))] + [shape(v.shape, v.dtype) for v in others],
        in_specs=[VM] * 11,
        out_specs=[VM] * 4,
        compiler_params=params(12),
        cost_estimate=cost(0, 6 << 20),
        name="stage",
    )(*pieces, *others)


def is_live(counts_ref):
    return counts_ref[lax.axis_index("fsdp")] > 0


def moments_kernel(counts_ref, *refs):
    pieces, (left_ref, right_ref, first_ref, second_ref) = refs[:8], refs[8:12]
    m_ref, v_ref, ln_ref, up_ref, g_ref = refs[12:]
    assemble(pieces, g_ref)
    rotated = contract(g_ref[...], right_ref[...], ((1,), (0,))).astype(BF)
    turned = contract(left_ref[...], rotated, ((0,), (0,)))
    moment = decay_first * first_ref[...].astype(F32) + (1.0 - decay_first) * turned
    second = decay_second * second_ref[...] + (1.0 - decay_second) * turned * turned
    normal = (moment / (jnp.sqrt(second) + epsilon)).astype(BF)
    back = contract(left_ref[...], normal, ((1,), (0,))).astype(BF)
    ln_ref[...] = back
    back_share(back, right_ref, 4, up_ref)
    live = is_live(counts_ref)
    m_ref[...] = jnp.where(live, moment.astype(BF), first_ref[...])
    v_ref[...] = jnp.where(live, second, second_ref[...])


def back_share(back, right_ref, distance, out):
    rows = lanes(place_of(distance, lax.axis_index("dp"), DP))
    out[...] = contract(back, right_ref[rows, :], ((1,), (1,))).astype(BF)


def moments(counts, pieces, left, right, first, second):
    size, share = right.shape
    kinds = (BF, F32, BF, BF)
    return pl.pallas_call(
        moments_kernel,
        out_shape=[shape((size, share), kind) for kind in kinds],
        in_specs=[SM] + [VM] * 12,
        out_specs=[VM] * 4,
        scratch_shapes=[pltpu.VMEM((size, size), BF)],
        compiler_params=params(20),
        cost_estimate=cost(6 * size * size * share, 7 << 20),
        name="moments",
    )(counts, *pieces, left, right, first, second)


LATER = (3, 5, 6, 2, 7, 1, 0)


def later_kernel(ln_ref, right_ref, *outs):
    for distance, out in zip(LATER, outs):
        back_share(ln_ref[...], right_ref, distance, out)


def later_shares(back, right):
    return pl.pallas_call(
        later_kernel,
        out_shape=[shape(back.shape)] * len(LATER),
        in_specs=[VM] * 2,
        out_specs=[VM] * len(LATER),
        compiler_params=params(8),
        cost_estimate=cost(2 * back.shape[0] ** 2 * back.shape[1], 2 << 20),
        name="later_shares",
    )(back, right)


def grams_kernel(counts_ref, *refs):
    pieces = refs[:8]
    left_ref, right_ref, new_left_ref, new_right_ref, g_ref = refs[8:]
    assemble(pieces, g_ref)
    d = lax.axis_index("dp")
    live = is_live(counts_ref)
    gram = contract(g_ref[...], g_ref[lanes(d), :], ((1,), (1,)))
    old = left_ref[...]
    new_left_ref[...] = jnp.where(live, decay_gram * old + (1.0 - decay_gram) * gram, old)
    gram = contract(g_ref[...], pieces[0][...], ((0,), (0,)))
    old = right_ref[...]
    new_right_ref[...] = jnp.where(live, decay_gram * old + (1.0 - decay_gram) * gram, old)


def grams(counts, pieces, left_stat, right_stat):
    size, share = left_stat.shape
    return pl.pallas_call(
        grams_kernel,
        out_shape=[shape((size, share), F32)] * 2,
        in_specs=[SM] + [VM] * 10,
        out_specs=[VM] * 2,
        scratch_shapes=[pltpu.VMEM((size, size), BF)],
        compiler_params=params(20),
        cost_estimate=cost(4 * size * size * share, 5 << 20),
        name="grams",
    )(counts, *pieces, left_stat, right_stat)


def fresh_kernel(owners_ref, weight_ref, back_ref, new_ref, key_ref):
    d = lax.axis_index("dp")
    for b in range(new_ref.shape[0]):
        old = weight_ref[b // 8, :, lanes((b % 8) * DP + d)].astype(F32)
        value = (old - step_size * back_ref[owners_ref[b]].astype(F32)).astype(BF)
        new_ref[b] = value
        if b < 8:
            key_ref[:, b * 128 : (b + 1) * 128] = value


def fresh_rows(owners, weight, back):
    rows = weight.shape[1]
    return pl.pallas_call(
        fresh_kernel,
        out_shape=[shape((16, rows, 128)), shape((rows, 1024))],
        in_specs=[SM, VM, VM],
        out_specs=[VM, VM],
        compiler_params=params(8),
        cost_estimate=cost(0, 2 << 20),
        name="fresh_rows",
    )(owners, weight, back)


def lay_kernel(*refs):
    pieces, outs = refs[:8], refs[8:]
    d = lax.axis_index("dp")
    for offset, ref in zip(RING, pieces):
        e = place_of(offset, d, DP)
        for c in range(8):
            outs[c // 4][:, lanes((c % 4) * DP + e)] = ref[:, c * 128 : (c + 1) * 128]


def lay(pieces):
    rows, wide = pieces[0].shape
    return pl.pallas_call(
        lay_kernel,
        out_shape=[shape((rows, 4 * wide))] * 2,
        in_specs=[VM] * 8,
        out_specs=[VM] * 2,
        compiler_params=params(4),
        cost_estimate=cost(0, 1 << 20),
        name="lay",
    )(*pieces)


def here():
    rank = lax.axis_index("fsdp")
    return lax.div(rank, SIDE * CORES), lax.rem(lax.div(rank, CORES), SIDE)


def rows_of(place, count=32):
    return pl.ds(pl.multiple_of(place * count, count), count)


def project_near_kernel(*refs):
    a_refs, b_refs, own_ref, other_ref, held = refs[:3], refs[3:6], *refs[6:9]
    outs, keys, sems = refs[9:11], *refs[11:]
    y, x = here()
    half = keys.shape[1] // 2
    copies = []
    for i, far in enumerate(FOUR[:3]):
        for j, near in enumerate(FOUR):
            place = place_of(far, y, SIDE) * SIDE + place_of(near, x, SIDE)
            to = keys.at[rows_of(place), :half]
            bring(a_refs[i].at[j * 32 : j * 32 + 32, :], to, sems, copies)
            place = place_of(near, y, SIDE) * SIDE + place_of(far, x, SIDE)
            to = keys.at[rows_of(place), half:]
            bring(b_refs[i].at[j * 32 : j * 32 + 32, :], to, sems, copies)
    bring(other_ref, held, sems, copies)
    nothing = jnp.zeros((32, half), BF)
    for j in range(SIDE):
        keys[rows_of(place_of(2, y, SIDE) * SIDE + j), :half] = nothing
        keys[rows_of(j * SIDE + place_of(2, x, SIDE)), half:] = nothing
    for copy in copies:
        copy.wait()
    for n in range(0, keys.shape[0], 256):
        for ref, out in zip((own_ref, held), outs):
            out[:, n : n + 256] = contract(ref[...], keys[n : n + 256, :], ((1,), (1,)))


def project_near(a, b, tokens):
    count, width = tokens[0].shape
    size = SIDE * SIDE * 32
    return pl.pallas_call(
        project_near_kernel,
        out_shape=[shape((count, width))] + [shape((count, size), F32)] * 2,
        in_specs=[ANY] * 6 + [VM, ANY],
        out_specs=[VM] * 3,
        scratch_shapes=[pltpu.VMEM((size, width), BF), pltpu.SemaphoreType.DMA((25,))],
        compiler_params=params(22),
        cost_estimate=cost(4 * count * width * size, 16 << 20),
        name="project_near",
    )(*a, *b, *tokens)


def project_far_kernel(*refs):
    far, tokens, sums, outs, (keys_a, keys_b) = refs[:4], refs[4:6], refs[6:8], refs[8:10], refs[10:]
    y, x = here()
    half = keys_a.shape[1]
    for rank, keys, parts in ((x, keys_a, far[:2]), (y, keys_b, far[2:])):
        for j, offset in enumerate(FOUR):
            row = (j % 2) * 32
            keys[rows_of(place_of(offset, rank, SIDE)), :] = parts[j // 2][row : row + 32, :]
    lane = lax.broadcasted_iota(jnp.int32, (tokens[0].shape[0], 128), 1)
    far_y, far_x = place_of(2, y, SIDE), place_of(2, x, SIDE)
    wanted = lax.div(lane, 32) == far_x
    for ref, total, out in zip(tokens, sums, outs):
        by_x = contract(ref[:, :half], keys_a[...], ((1,), (1,)))
        by_y = contract(ref[:, half:], keys_b[...], ((1,), (1,)))
        for j in range(SIDE):
            moved = pltpu.roll(by_y, lax.rem(far_x + (SIDE - j), SIDE) * 32, 1)
            value = total[:, j * 128 : j * 128 + 128] + jnp.where(wanted, moved, 0.0)
            value += jnp.where(far_y == j, by_x, 0.0)
            out[:, j * 128 : j * 128 + 128] = value.astype(BF)


def project_far(far, tokens, sums):
    count, width = tokens[0].shape
    size = sums[0].shape[1]
    return pl.pallas_call(
        project_far_kernel,
        out_shape=[shape((count, size))] * 2,
        in_specs=[VM] * 8,
        out_specs=[VM] * 2,
        scratch_shapes=[pltpu.VMEM((128, width // 2), BF)] * 2,
        compiler_params=params(16),
        cost_estimate=cost(count * width * size, 4 << 20),
        name="project_far",
    )(*far, *tokens, *sums)


def on_device(
    tokens,
    gradients,
    weight,
    owners,
    counts,
    left_basis,
    right_basis,
    left_stat,
    right_stat,
    first_moment,
    second_moment,
):
    row_share = weight.shape[1]
    block_size, col_share = left_basis.shape[2:]
    left_local, right_local = left_basis[0, 0], right_basis[0, 0]

    grad = gradients[0]
    shares_of = dict(zip((4, *LATER), (*shares(grad, (4,)), *shares(grad, LATER))))
    first_left = along_dp(left_local, 1), along_dp(left_local, -1)
    up, down, done = ring_sum(shares_of, {2: first_left})
    first_left = done[2]
    second_left = along_dp(first_left[0], 1), along_dp(first_left[1], -1)
    up, down, second_left = lax.optimization_barrier((up, down, second_left))
    third_left = along_dp(second_left[0], 1), along_dp(second_left[1], -1)
    packed = pack(owners, shares_of[0], up, down)

    arrived = lax.all_to_all(packed, "fsdp", split_axis=0, concat_axis=0, tiled=True)
    arrived = arrived.reshape(block_size, col_share)
    last_left = along_dp(third_left[1], -1)
    pieces, done = ring_gather(arrived, {1: third_left, 3: last_left})
    lefts = [left_local, first_left[0], second_left[0], done[1][0], done[3]]
    lefts += [first_left[1], second_left[1], done[1][1]]
    left_full, right, first, second = stage(
        lefts, right_local, first_moment[0, 0], second_moment[0, 0]
    )
    new_first, new_second, back, farthest = moments(counts, pieces, left_full, right, first, second)
    shares_of = dict(zip((4, *LATER), (farthest, *later_shares(back, right))))
    up, down, done = ring_sum(shares_of, {1: in_plane(tokens, "core", 1)})
    other = done[1]
    update = (shares_of[0].astype(F32) + up.astype(F32) + down.astype(F32)).astype(BF)
    returned = lax.all_to_all(
        update.reshape(FSDP, row_share, col_share), "fsdp", split_axis=0, concat_axis=0, tiled=True
    )
    new_rows, key_rows = fresh_rows(owners, weight, returned)
    new_weight = new_rows.reshape(2, 8, row_share, col_share).transpose(0, 2, 1, 3)

    part_a, part_b = lay(ring_gather(key_rows, {})[0])
    part_a = jnp.concatenate(four_gather(part_a, "x"), 0)
    part_b = jnp.concatenate(four_gather(part_b, "y"), 0)
    part_a, part_b = lax.optimization_barrier((part_a, part_b))
    stats = grams(counts, pieces, left_stat[0, 0], right_stat[0, 0])
    near_a = in_plane(part_a, "y", 1), in_plane(part_a, "y", -1)
    near_b = in_plane(part_b, "x", 1), in_plane(part_b, "x", -1)
    near_a, near_b, stats = lax.optimization_barrier((near_a, near_b, stats))
    new_left, new_right = stats
    half = part_a.shape[0] // 2
    far_a = in_plane(near_a[0][:half], "y", 1), in_plane(near_a[1][half:], "y", -1)
    far_b = in_plane(near_b[0][:half], "x", 1), in_plane(near_b[1][half:], "x", -1)
    other, *sums = project_near((part_a, *near_a), (part_b, *near_b), (tokens, other))
    tokens = (tokens, other)
    mine, theirs = project_far((*far_a, *far_b), tokens, sums)
    got = in_plane(theirs, "core", 1)
    core = lax.rem(lax.axis_index("fsdp"), CORES)
    even = jnp.where(core == 0, mine, got)
    odd = jnp.where(core == 0, got, mine)
    count = tokens[0].shape[0]
    projected = jnp.stack(
        [even.reshape(count, SIDE * SIDE, row_share), odd.reshape(count, SIDE * SIDE, row_share)], 2
    ).reshape(count, SIDE * SIDE * CORES * row_share)
    return (
        projected,
        new_weight,
        new_left[None, None],
        new_right[None, None],
        new_first[None, None],
        new_second[None, None],
    )


def solution(mesh):
    state = P("fsdp", None, None, "dp")
    return jax.shard_map(
        on_device,
        mesh=mesh,
        in_specs=(
            P(("dp", "fsdp"), None),
            P("dp", None, "fsdp", None),
            P(None, "fsdp", None),
            P(),
            P(),
            state,
            state,
            state,
            state,
            state,
            state,
        ),
        out_specs=(
            P(("dp", "fsdp"), None),
            P(None, "fsdp", None, "dp"),
            state,
            state,
            state,
            state,
        ),
        check_vma=False,
    )
```

```python
import functools

import jax
import jax.numpy as jnp
from jax import lax
from jax.experimental import pallas as pl
from jax.experimental.pallas import tpu as pltpu
from jax.sharding import PartitionSpec as P

step_size = 0.02
decay_first = 0.9
decay_second = 0.95
decay_gram = 0.95
epsilon = 1e-08

BF = jnp.bfloat16
F32 = jnp.float32
DP = 8
SIDE = 4
CORES = 2
FSDP = SIDE * SIDE * CORES
RING = (0, -1, -2, -3, 4, 1, 2, 3)
FOUR = (0, -1, 1, 2)


def params(mebibytes):
    return pltpu.CompilerParams(vmem_limit_bytes=mebibytes << 20)


def cost(flops, moved):
    return pl.CostEstimate(flops=flops, bytes_accessed=moved, transcendentals=0)


def shape(dims, kind=BF):
    return jax.ShapeDtypeStruct(dims, kind)


VM = pl.BlockSpec(memory_space=pltpu.VMEM)
SM = pl.BlockSpec(memory_space=pltpu.SMEM)
HBM = pl.BlockSpec(memory_space=pltpu.HBM)
ANY = pl.BlockSpec(memory_space=pl.ANY)


def along_dp(value, by):
    return lax.ppermute(value, "dp", [(i, (i + by) % DP) for i in range(DP)])


def in_plane(value, axis, by):
    pairs = []
    for i in range(FSDP):
        y, x, c = i // (SIDE * CORES), (i // CORES) % SIDE, i % CORES
        if axis == "x":
            x = (x + by) % SIDE
        elif axis == "y":
            y = (y + by) % SIDE
        else:
            c = (c + by) % CORES
        pairs.append((i, (y * SIDE + x) * CORES + c))
    return lax.ppermute(value, "fsdp", pairs)


def ring_gather(piece, beside):
    up, down, done = [piece], [piece], {}
    for step in range(4):
        if step in beside:
            up[-1], down[-1], done[step] = lax.optimization_barrier(
                (up[-1], down[-1], beside[step])
            )
        up.append(along_dp(up[-1], 1))
        if step > 0:
            down.append(along_dp(down[-1], -1))
    return up + down[1:], done


def four_gather(value, axis):
    half = value.shape[0] // 2
    a, b = in_plane(value, axis, 1), in_plane(value, axis, -1)
    return [value, a, b, in_plane(a[:half], axis, 1), in_plane(b[half:], axis, -1)]


def place_of(offset, rank, count):
    return lax.rem(rank + (offset + count), count)


def lanes(index, width=128):
    return pl.ds(pl.multiple_of(index * width, width), width)


def shares_kernel(wanted, g_ref, *outs):
    d = lax.axis_index("dp")
    for k, out in zip(wanted, outs):
        e = place_of(k, d, DP)
        for b in range(out.shape[0]):
            out[b] = g_ref[b // 8, :, lanes((b % 8) * DP + e)]


def shares(g, wanted):
    rows = g.shape[1]
    return pl.pallas_call(
        functools.partial(shares_kernel, wanted),
        out_shape=[shape((16, rows, 128))] * len(wanted),
        in_specs=[VM],
        out_specs=[VM] * len(wanted),
        compiler_params=params(8),
        cost_estimate=cost(0, 2 << 20),
        name="shares",
    )(g)


def pack_kernel(owners_ref, own_ref, up_ref, down_ref, out_ref):
    out_ref[...] = jnp.zeros_like(out_ref)
    for b in range(own_ref.shape[0]):
        total = own_ref[b].astype(F32) + up_ref[b].astype(F32) + down_ref[b].astype(F32)
        out_ref[owners_ref[b]] = total.astype(BF)


def pack(owners, own, up, down):
    return pl.pallas_call(
        pack_kernel,
        out_shape=shape((FSDP,) + own.shape[1:]),
        in_specs=[SM, VM, VM, VM],
        out_specs=VM,
        compiler_params=params(4),
        cost_estimate=cost(0, 1 << 20),
        name="pack",
    )(owners, own, up, down)


def add(a, b):
    return (a.astype(F32) + b.astype(F32)).astype(BF)


def ring_sum(shares_of, beside):
    up, down, done = add(shares_of[3], along_dp(shares_of[4], 1)), shares_of[5], {}
    for step, a, b in ((1, 2, 6), (2, 1, 7), (3, None, None)):
        if step in beside:
            up, down, done[step] = lax.optimization_barrier((up, down, beside[step]))
        up, down = along_dp(up, 1), along_dp(down, -1)
        if a is not None:
            up, down = add(shares_of[a], up), add(shares_of[b], down)
    return up, down, done


def bring(ref, to, sems, copies):
    copies.append(pltpu.make_async_copy(ref, to, sems.at[len(copies)]))
    copies[-1].start()


def assemble(pieces, out):
    d = lax.axis_index("dp")
    for offset, ref in zip(RING, pieces):
        out[:, lanes(place_of(offset, d, DP))] = ref[...]


def contract(a, b, dims):
    return lax.dot_general(a, b, (dims, ((), ())), preferred_element_type=F32)


EARLY, LATE = (0, -1, -2, -3, 1, 2), (4, 3)


def rotated_by(offsets, pieces, right_ref):
    d = lax.axis_index("dp")
    total = 0.0
    for offset, ref in zip(offsets, pieces):
        rows = right_ref[lanes(place_of(offset, d, DP)), :]
        total += contract(ref[...], rows, ((1,), (0,)))
    return total


def stage_kernel(*refs):
    lefts, others, early, (left_ref, *outs, part_ref) = refs[:8], refs[8:11], refs[11:17], refs[17:]
    assemble(lefts, left_ref)
    for ref, out in zip(others, outs):
        out[...] = ref[...]
    part_ref[...] = rotated_by(EARLY, early, others[0])


def stage(pieces, others, early):
    size = pieces[0].shape[0]
    return pl.pallas_call(
        stage_kernel,
        out_shape=[shape((size, size))]
        + [shape(v.shape, v.dtype) for v in others]
        + [shape(pieces[0].shape, F32)],
        in_specs=[VM] * 17,
        out_specs=[VM] * 5,
        compiler_params=params(12),
        cost_estimate=cost(0, 6 << 20),
        name="stage",
    )(*pieces, *others, *early)


def is_live(counts_ref):
    return counts_ref[lax.axis_index("fsdp")] > 0


def moments_kernel(counts_ref, *refs):
    late, (part_ref, left_ref, right_ref, first_ref, second_ref) = refs[:2], refs[2:7]
    m_ref, v_ref, ln_ref, up_ref = refs[7:]
    rotated = (part_ref[...] + rotated_by(LATE, late, right_ref)).astype(BF)
    turned = contract(left_ref[...], rotated, ((0,), (0,)))
    moment = decay_first * first_ref[...].astype(F32) + (1.0 - decay_first) * turned
    second = decay_second * second_ref[...] + (1.0 - decay_second) * turned * turned
    normal = (moment / (jnp.sqrt(second) + epsilon)).astype(BF)
    back = contract(left_ref[...], normal, ((1,), (0,))).astype(BF)
    ln_ref[...] = back
    back_share(back, right_ref, 4, up_ref)
    live = is_live(counts_ref)
    m_ref[...] = jnp.where(live, moment.astype(BF), first_ref[...])
    v_ref[...] = jnp.where(live, second, second_ref[...])


def back_share(back, right_ref, distance, out):
    rows = lanes(place_of(distance, lax.axis_index("dp"), DP))
    out[...] = contract(back, right_ref[rows, :], ((1,), (1,))).astype(BF)


def moments(counts, late, part, left, right, first, second):
    size, share = right.shape
    kinds = (BF, F32, BF, BF)
    return pl.pallas_call(
        moments_kernel,
        out_shape=[shape((size, share), kind) for kind in kinds],
        in_specs=[SM] + [VM] * 7,
        out_specs=[VM] * 4,
        compiler_params=params(20),
        cost_estimate=cost(6 * size * size * share, 7 << 20),
        name="moments",
    )(counts, *late, part, left, right, first, second)


LATER = (3, 5, 6, 2, 7, 1, 0)


def later_kernel(ln_ref, right_ref, *outs):
    for distance, out in zip(LATER, outs):
        back_share(ln_ref[...], right_ref, distance, out)


def later_shares(back, right):
    return pl.pallas_call(
        later_kernel,
        out_shape=[shape(back.shape)] * len(LATER),
        in_specs=[VM] * 2,
        out_specs=[VM] * len(LATER),
        compiler_params=params(8),
        cost_estimate=cost(2 * back.shape[0] ** 2 * back.shape[1], 2 << 20),
        name="later_shares",
    )(back, right)


def grams_kernel(counts_ref, *refs):
    pieces = refs[:8]
    left_ref, right_ref, new_left_ref, new_right_ref, g_ref = refs[8:]
    assemble(pieces, g_ref)
    d = lax.axis_index("dp")
    live = is_live(counts_ref)
    gram = contract(g_ref[...], g_ref[lanes(d), :], ((1,), (1,)))
    old = left_ref[...]
    new_left_ref[...] = jnp.where(live, decay_gram * old + (1.0 - decay_gram) * gram, old)
    gram = contract(g_ref[...], pieces[0][...], ((0,), (0,)))
    old = right_ref[...]
    new_right_ref[...] = jnp.where(live, decay_gram * old + (1.0 - decay_gram) * gram, old)


def grams(counts, pieces, left_stat, right_stat):
    size, share = left_stat.shape
    return pl.pallas_call(
        grams_kernel,
        out_shape=[shape((size, share), F32)] * 2,
        in_specs=[SM] + [VM] * 10,
        out_specs=[VM] * 2,
        scratch_shapes=[pltpu.VMEM((size, size), BF)],
        compiler_params=params(20),
        cost_estimate=cost(4 * size * size * share, 5 << 20),
        name="grams",
    )(counts, *pieces, left_stat, right_stat)


def fresh_kernel(owners_ref, weight_ref, back_ref, new_ref, key_ref):
    d = lax.axis_index("dp")
    for b in range(new_ref.shape[0]):
        old = weight_ref[b // 8, :, lanes((b % 8) * DP + d)].astype(F32)
        value = (old - step_size * back_ref[owners_ref[b]].astype(F32)).astype(BF)
        new_ref[b] = value
        if b < 8:
            key_ref[:, b * 128 : (b + 1) * 128] = value


def fresh_rows(owners, weight, back):
    rows = weight.shape[1]
    return pl.pallas_call(
        fresh_kernel,
        out_shape=[shape((16, rows, 128)), shape((rows, 1024))],
        in_specs=[SM, VM, VM],
        out_specs=[VM, VM],
        compiler_params=params(8),
        cost_estimate=cost(0, 2 << 20),
        name="fresh_rows",
    )(owners, weight, back)


def lay_kernel(*refs):
    pieces, outs = refs[:8], refs[8:]
    d = lax.axis_index("dp")
    for offset, ref in zip(RING, pieces):
        e = place_of(offset, d, DP)
        for c in range(8):
            outs[c // 4][:, lanes((c % 4) * DP + e)] = ref[:, c * 128 : (c + 1) * 128]


def lay(pieces):
    rows, wide = pieces[0].shape
    return pl.pallas_call(
        lay_kernel,
        out_shape=[shape((rows, 4 * wide))] * 2,
        in_specs=[VM] * 8,
        out_specs=[VM] * 2,
        compiler_params=params(4),
        cost_estimate=cost(0, 1 << 20),
        name="lay",
    )(*pieces)


def here():
    rank = lax.axis_index("fsdp")
    return lax.div(rank, SIDE * CORES), lax.rem(lax.div(rank, CORES), SIDE)


def rows_of(place, count=32):
    return pl.ds(pl.multiple_of(place * count, count), count)


def project_near_kernel(*refs):
    a_refs, b_refs, own_ref, other_ref, held = refs[:3], refs[3:6], *refs[6:9]
    outs, keys, sems = refs[9:11], *refs[11:]
    y, x = here()
    half = keys.shape[1] // 2
    copies = []
    for i, far in enumerate(FOUR[:3]):
        for j, near in enumerate(FOUR):
            place = place_of(far, y, SIDE) * SIDE + place_of(near, x, SIDE)
            to = keys.at[rows_of(place), :half]
            bring(a_refs[i].at[j * 32 : j * 32 + 32, :], to, sems, copies)
            place = place_of(near, y, SIDE) * SIDE + place_of(far, x, SIDE)
            to = keys.at[rows_of(place), half:]
            bring(b_refs[i].at[j * 32 : j * 32 + 32, :], to, sems, copies)
    bring(other_ref, held, sems, copies)
    nothing = jnp.zeros((32, half), BF)
    for j in range(SIDE):
        keys[rows_of(place_of(2, y, SIDE) * SIDE + j), :half] = nothing
        keys[rows_of(j * SIDE + place_of(2, x, SIDE)), half:] = nothing
    for copy in copies:
        copy.wait()
    for n in range(0, keys.shape[0], 256):
        for ref, out in zip((own_ref, held), outs):
            out[:, n : n + 256] = contract(ref[...], keys[n : n + 256, :], ((1,), (1,)))


def project_near(a, b, tokens):
    count, width = tokens[0].shape
    size = SIDE * SIDE * 32
    return pl.pallas_call(
        project_near_kernel,
        out_shape=[shape((count, width))] + [shape((count, size), F32)] * 2,
        in_specs=[ANY] * 6 + [VM, ANY],
        out_specs=[VM] * 3,
        scratch_shapes=[pltpu.VMEM((size, width), BF), pltpu.SemaphoreType.DMA((25,))],
        compiler_params=params(22),
        cost_estimate=cost(4 * count * width * size, 16 << 20),
        name="project_near",
    )(*a, *b, *tokens)


def project_far_kernel(*refs):
    far, tokens, sums, outs, (keys_a, keys_b) = refs[:4], refs[4:6], refs[6:8], refs[8:10], refs[10:]
    y, x = here()
    half = keys_a.shape[1]
    for rank, keys, parts in ((x, keys_a, far[:2]), (y, keys_b, far[2:])):
        for j, offset in enumerate(FOUR):
            row = (j % 2) * 32
            keys[rows_of(place_of(offset, rank, SIDE)), :] = parts[j // 2][row : row + 32, :]
    lane = lax.broadcasted_iota(jnp.int32, (tokens[0].shape[0], 128), 1)
    far_y, far_x = place_of(2, y, SIDE), place_of(2, x, SIDE)
    wanted = lax.div(lane, 32) == far_x
    for ref, total, out in zip(tokens, sums, outs):
        by_x = contract(ref[:, :half], keys_a[...], ((1,), (1,)))
        by_y = contract(ref[:, half:], keys_b[...], ((1,), (1,)))
        for j in range(SIDE):
            moved = pltpu.roll(by_y, lax.rem(far_x + (SIDE - j), SIDE) * 32, 1)
            value = total[:, j * 128 : j * 128 + 128] + jnp.where(wanted, moved, 0.0)
            value += jnp.where(far_y == j, by_x, 0.0)
            out[:, j * 128 : j * 128 + 128] = value.astype(BF)


def project_far(far, tokens, sums):
    count, width = tokens[0].shape
    size = sums[0].shape[1]
    return pl.pallas_call(
        project_far_kernel,
        out_shape=[shape((count, size))] * 2,
        in_specs=[VM] * 8,
        out_specs=[VM] * 2,
        scratch_shapes=[pltpu.VMEM((128, width // 2), BF)] * 2,
        compiler_params=params(16),
        cost_estimate=cost(count * width * size, 4 << 20),
        name="project_far",
    )(*far, *tokens, *sums)


def on_device(
    tokens,
    gradients,
    weight,
    owners,
    counts,
    left_basis,
    right_basis,
    left_stat,
    right_stat,
    first_moment,
    second_moment,
):
    row_share = weight.shape[1]
    block_size, col_share = left_basis.shape[2:]
    left_local, right_local = left_basis[0, 0], right_basis[0, 0]

    grad = gradients[0]
    shares_of = dict(zip((4, *LATER), (*shares(grad, (4,)), *shares(grad, LATER))))
    first_left = along_dp(left_local, 1), along_dp(left_local, -1)
    up, down, done = ring_sum(shares_of, {2: first_left})
    first_left = done[2]
    second_left = along_dp(first_left[0], 1), along_dp(first_left[1], -1)
    up, down, second_left = lax.optimization_barrier((up, down, second_left))
    third_left = along_dp(second_left[0], 1), along_dp(second_left[1], -1)
    packed = pack(owners, shares_of[0], up, down)

    arrived = lax.all_to_all(packed, "fsdp", split_axis=0, concat_axis=0, tiled=True)
    arrived = arrived.reshape(block_size, col_share)
    last_left = along_dp(third_left[1], -1)
    pieces, done = ring_gather(arrived, {1: third_left, 3: last_left})
    lefts = [left_local, first_left[0], second_left[0], done[1][0], done[3]]
    lefts += [first_left[1], second_left[1], done[1][1]]
    placed = dict(zip(RING, pieces))
    left_full, right, first, second, part = stage(
        lefts,
        (right_local, first_moment[0, 0], second_moment[0, 0]),
        [placed[k] for k in EARLY],
    )
    new_first, new_second, back, farthest = moments(
        counts, [placed[k] for k in LATE], part, left_full, right, first, second
    )
    shares_of = dict(zip((4, *LATER), (farthest, *later_shares(back, right))))
    up, down, done = ring_sum(shares_of, {1: in_plane(tokens, "core", 1)})
    other = done[1]
    update = (shares_of[0].astype(F32) + up.astype(F32) + down.astype(F32)).astype(BF)
    returned = lax.all_to_all(
        update.reshape(FSDP, row_share, col_share), "fsdp", split_axis=0, concat_axis=0, tiled=True
    )
    new_rows, key_rows = fresh_rows(owners, weight, returned)
    new_weight = new_rows.reshape(2, 8, row_share, col_share).transpose(0, 2, 1, 3)

    part_a, part_b = lay(ring_gather(key_rows, {})[0])
    part_a = jnp.concatenate(four_gather(part_a, "x"), 0)
    part_b = jnp.concatenate(four_gather(part_b, "y"), 0)
    part_a, part_b = lax.optimization_barrier((part_a, part_b))
    stats = grams(counts, pieces, left_stat[0, 0], right_stat[0, 0])
    near_a = in_plane(part_a, "y", 1), in_plane(part_a, "y", -1)
    near_b = in_plane(part_b, "x", 1), in_plane(part_b, "x", -1)
    near_a, near_b, stats = lax.optimization_barrier((near_a, near_b, stats))
    new_left, new_right = stats
    half = part_a.shape[0] // 2
    far_a = in_plane(near_a[0][:half], "y", 1), in_plane(near_a[1][half:], "y", -1)
    far_b = in_plane(near_b[0][:half], "x", 1), in_plane(near_b[1][half:], "x", -1)
    other, *sums = project_near((part_a, *near_a), (part_b, *near_b), (tokens, other))
    tokens = (tokens, other)
    mine, theirs = project_far((*far_a, *far_b), tokens, sums)
    got = in_plane(theirs, "core", 1)
    core = lax.rem(lax.axis_index("fsdp"), CORES)
    even = jnp.where(core == 0, mine, got)
    odd = jnp.where(core == 0, got, mine)
    count = tokens[0].shape[0]
    projected = jnp.stack(
        [even.reshape(count, SIDE * SIDE, row_share), odd.reshape(count, SIDE * SIDE, row_share)], 2
    ).reshape(count, SIDE * SIDE * CORES * row_share)
    return (
        projected,
        new_weight,
        new_left[None, None],
        new_right[None, None],
        new_first[None, None],
        new_second[None, None],
    )


def solution(mesh):
    state = P("fsdp", None, None, "dp")
    return jax.shard_map(
        on_device,
        mesh=mesh,
        in_specs=(
            P(("dp", "fsdp"), None),
            P("dp", None, "fsdp", None),
            P(None, "fsdp", None),
            P(),
            P(),
            state,
            state,
            state,
            state,
            state,
            state,
        ),
        out_specs=(
            P(("dp", "fsdp"), None),
            P(None, "fsdp", None, "dp"),
            state,
            state,
            state,
            state,
        ),
        check_vma=False,
    )
```
